32 devices in a mesh: ctx: 8 (over y, x, core), fsdp: 4 (over z).
Axes of the slice: x: 2, y: 2, z: 4, core: 2. Of those that a mesh axis runs over, the one named last changes fastest.
Arguments:
- tokens: bfloat16 [16, 1024, 576], P('fsdp', 'ctx'), may hold values from -6 to 6
- block_order: int32 [16], replicated, may hold values from 0 to 15, each once
- gain_one: bfloat16 [576], P('fsdp'), may hold values from 0.5 to 1.5
- gain_two: bfloat16 [576], P('fsdp'), may hold values from 0.5 to 1.5
- query_weight: bfloat16 [576, 576], P('fsdp'), may hold values from -0.5 to 0.5
- key_matrix: bfloat16 [576, 192], P('fsdp'), may hold values from -0.25 to 0.25
- value_matrix: bfloat16 [576, 192], P('fsdp'), may hold values from -0.25 to 0.25
- out_weight: bfloat16 [576, 576], P('fsdp'), may hold values from -1.5 to 1.5
- gate_weight: bfloat16 [576, 1536], P('fsdp'), may hold values from -0.25 to 0.25
- up_weight: bfloat16 [576, 1536], P('fsdp'), may hold values from -0.25 to 0.25
- down_weight: bfloat16 [1536, 576], P('fsdp'), may hold values from -0.3125 to 0.3125
- cotangent: bfloat16 [16, 1024, 576], P('fsdp', 'ctx'), may hold values from -6 to 6
Outputs:
- output: bfloat16 [16, 1024, 576], P('fsdp', 'ctx')
- grad_tokens: bfloat16 [16, 1024, 576], P('fsdp', 'ctx')
- gain_one_grad: float32 [576], P('fsdp')
- gain_two_grad: float32 [576], P('fsdp')
- query_weight_grad: float32 [576, 576], P('fsdp')
- key_weight_grad: float32 [576, 192], P('fsdp')
- value_weight_grad: float32 [576, 192], P('fsdp')
- out_weight_grad: float32 [576, 576], P('fsdp')
- gate_weight_grad: float32 [576, 1536], P('fsdp')
- up_weight_grad: float32 [576, 1536], P('fsdp')
- down_weight_grad: float32 [1536, 576], P('fsdp')
The draws below stay inside these ranges and needn't reach their ends.
Inputs may be any that keep to these rules, and one draw needn't show every extreme that they name: A permutation; stored half-block j of every sequence (rows j * 64 to (j + 1) * 64 - 1) holds the tokens of positions block_order[j] * 64 onward.
All inputs are finite; a program needn't handle non-finite values.
Results may differ from the reference program's by a relative error of at most 0.02.
Values may be sent and summed in bfloat16 or wider, within the bound.
A program may use at most 256 MiB of HBM per device.

```python
import math
import jax
import jax.numpy as jnp
from jax import lax

MODEL_DIMENSION = 576
QUERY_HEADS = 9
KEY_VALUE_HEADS = 3
HEAD_DIMENSION = 64
FF = 1536
HALF = 64
SEQS = 16
SEQUENCE_LENGTH = 1024
N_CTX = 8


def block_scale(own_key, dims, pieces, low, high):
    def one(dim, parts):
        draws = jax.random.uniform(jax.random.fold_in(jax.random.fold_in(own_key, 6), dim), (parts,), jnp.float32, low / len(pieces), high / len(pieces))
        return jnp.repeat(jnp.exp(draws), dims[dim] // parts).reshape((-1,) + (1,) * (len(dims) - dim - 1))

    loudness = one(*pieces[0])
    for cut in pieces[1:]:
        loudness = loudness * one(*cut)
    return loudness


def centred(stream_key, dims, spread, limit, cuts=(), kind=jnp.bfloat16):
    factor_of = block_scale(stream_key, dims, cuts, -0.22, 0.18) if cuts else 1.0
    entries = jax.random.normal(stream_key, dims, jnp.float32) * spread * factor_of
    return jnp.minimum(jnp.maximum(entries, -limit), limit).astype(kind)


def setup_inputs(seed: int = 0) -> dict:
    streams_of = jax.random.split(jax.random.key(seed), 13)
    return {
        "tokens": centred(streams_of[0], (SEQS, SEQUENCE_LENGTH, MODEL_DIMENSION), 1.0, 6.0, ((0, 4), (1, 8))),
        "block_order": jax.random.permutation(streams_of[1], 2 * N_CTX).astype(jnp.int32),
        "gain_one": jnp.clip(1.0 + 0.1 * jax.random.normal(streams_of[2], (MODEL_DIMENSION,), jnp.float32), 0.5, 1.5).astype(jnp.bfloat16),
        "gain_two": jnp.clip(1.0 + 0.1 * jax.random.normal(streams_of[3], (MODEL_DIMENSION,), jnp.float32), 0.5, 1.5).astype(jnp.bfloat16),
        "query_weight": centred(streams_of[4], (MODEL_DIMENSION, QUERY_HEADS * HEAD_DIMENSION), (MODEL_DIMENSION // 4) ** -0.5, 0.5, ((0, 4),)),
        "key_matrix": centred(streams_of[5], (MODEL_DIMENSION, KEY_VALUE_HEADS * HEAD_DIMENSION), MODEL_DIMENSION ** -0.5, 0.25, ((0, 4),)),
        "value_matrix": centred(streams_of[6], (MODEL_DIMENSION, KEY_VALUE_HEADS * HEAD_DIMENSION), MODEL_DIMENSION ** -0.5, 0.25, ((0, 4),)),
        "out_weight": centred(streams_of[7], (QUERY_HEADS * HEAD_DIMENSION, MODEL_DIMENSION), 16 ** -0.5, 1.5, ((0, 4),)),
        "gate_weight": centred(streams_of[8], (MODEL_DIMENSION, FF), MODEL_DIMENSION ** -0.5, 0.25, ((0, 4),)),
        "up_weight": centred(streams_of[9], (MODEL_DIMENSION, FF), MODEL_DIMENSION ** -0.5, 0.25, ((0, 4),)),
        "down_weight": centred(streams_of[10], (FF, MODEL_DIMENSION), (FF // 4) ** -0.5, 0.3125, ((0, 4),)),
        "cotangent": centred(streams_of[11], (SEQS, SEQUENCE_LENGTH, MODEL_DIMENSION), 1.0, 6.0, ((0, 4), (1, 8))),
    }


@jax.custom_vjp
def lower_bound(v):
    return lax.optimization_barrier(v.astype(jnp.bfloat16)).astype(jnp.float32)

@jax.custom_vjp
def low_back(v):
    return v

def low_keep(v):
    return (lower_bound(v), None)

def low_pass(kept, grad):
    return (grad,)

def back_keep(v):
    return (v, None)

def back_low(kept, grad):
    return (lower_bound(grad),)
lower_bound.defvjp(low_keep, low_pass)
low_back.defvjp(back_keep, back_low)
eps = 1e-05
rope_base = 100000.0
mask_fill_value = -1e+30
highest = lax.Precision.HIGHEST

def positions_of(block_order):
    row_ids = jnp.arange(SEQUENCE_LENGTH, dtype=jnp.int32)
    return block_order[row_ids // HALF] * HALF + row_ids % HALF

def rope_tables(token_positions):
    inverse = jnp.exp(jnp.arange(HEAD_DIMENSION // 2, dtype=jnp.float32) * (-2.0 * math.log(rope_base) / HEAD_DIMENSION))
    angles = token_positions.astype(jnp.float32)[:, None] * inverse[None, :]
    return (jnp.cos(angles), jnp.sin(angles))

def apply_rotary(vectors, cosine_table, sine_table):
    front = vectors[..., :HEAD_DIMENSION // 2]
    back_half = vectors[..., HEAD_DIMENSION // 2:]
    cos_rows = cosine_table[:, None, :]
    sin_rows = sine_table[:, None, :]
    return jnp.concatenate([front * cos_rows - back_half * sin_rows, back_half * cos_rows + front * sin_rows], axis=-1)

def attention_output(query_rows_all, keys_all, values_all, token_positions):
    rows_per_block = min(512, SEQUENCE_LENGTH)
    count_of_blocks = SEQUENCE_LENGTH // rows_per_block
    score_scale = HEAD_DIMENSION ** (-0.5)
    blocks_of_queries = query_rows_all.reshape(count_of_blocks, rows_per_block, KEY_VALUE_HEADS, QUERY_HEADS // KEY_VALUE_HEADS, HEAD_DIMENSION)
    position_blocks = token_positions.reshape(count_of_blocks, rows_per_block)

    def one_block(block_item):
        query_part, query_positions = block_item
        scores = jnp.einsum('qhgd,khd->hgqk', query_part, keys_all, precision=highest) * score_scale
        scores = low_back(scores)
        allowed = query_positions[:, None] >= token_positions[None, :]
        masked = jnp.where(allowed, scores, mask_fill_value)
        row_top = lax.optimization_barrier(jnp.max(masked, axis=-1, keepdims=True))
        exponent = jnp.where(allowed, jnp.exp(masked - row_top), 0.0)
        probability = exponent / lax.optimization_barrier(jnp.sum(exponent, axis=-1, keepdims=True))
        return jnp.einsum('hgqk,khd->qhgd', lower_bound(probability), values_all, precision=highest)
    mixed_heads = lax.map(jax.checkpoint(one_block), (blocks_of_queries, position_blocks))
    return mixed_heads.reshape(SEQUENCE_LENGTH, QUERY_HEADS * HEAD_DIMENSION)

def rms_scale(values_in):
    return lax.rsqrt(lax.optimization_barrier(jnp.mean(values_in * values_in, axis=-1, keepdims=True)) + eps)

def layer(sequence, gain_one, gain_two, query_weight, key_matrix, value_matrix, out_weight, gate_weight, up_weight, down_weight, cosine_table, sine_table, token_positions):
    normed = lower_bound(sequence * rms_scale(sequence) * gain_one)
    query_rows_all = low_back(jnp.dot(normed, query_weight, precision=highest))
    projected_key = low_back(jnp.dot(normed, key_matrix, precision=highest))
    projected_value = lower_bound(low_back(jnp.dot(normed, value_matrix, precision=highest)))
    rotary_query = lower_bound(apply_rotary(query_rows_all.reshape(SEQUENCE_LENGTH, QUERY_HEADS, HEAD_DIMENSION), cosine_table, sine_table)).reshape(SEQUENCE_LENGTH, KEY_VALUE_HEADS, QUERY_HEADS // KEY_VALUE_HEADS, HEAD_DIMENSION)
    rotary_key = lower_bound(apply_rotary(projected_key.reshape(SEQUENCE_LENGTH, KEY_VALUE_HEADS, HEAD_DIMENSION), cosine_table, sine_table))
    mixed_heads = attention_output(rotary_query, rotary_key, projected_value.reshape(SEQUENCE_LENGTH, KEY_VALUE_HEADS, HEAD_DIMENSION), token_positions)
    mixed_heads = lower_bound(low_back(mixed_heads))
    middle = sequence + low_back(jnp.dot(mixed_heads, out_weight, precision=highest))
    normed_two = lower_bound(middle * rms_scale(middle) * gain_two)
    gate_proj = low_back(jnp.dot(normed_two, gate_weight, precision=highest))
    up_proj = low_back(jnp.dot(normed_two, up_weight, precision=highest))
    hidden = lower_bound(jax.nn.silu(gate_proj) * up_proj)
    return middle + jnp.dot(hidden, down_weight, precision=highest)

def reference(tokens, block_order, gain_one, gain_two, query_weight, key_matrix, value_matrix, out_weight, gate_weight, up_weight, down_weight, cotangent):
    token_positions = positions_of(block_order)
    cosine_table, sine_table = rope_tables(token_positions)
    weights = tuple((w_item.astype(jnp.float32) for w_item in (gain_one, gain_two, query_weight, key_matrix, value_matrix, out_weight, gate_weight, up_weight, down_weight)))

    def per_sequence(totals, seq_item):
        sequence, cotangent_row = seq_item

        def forward(sequence_in, *params):
            return layer(sequence_in, *params, cosine_table, sine_table, token_positions)
        result, pullback = jax.vjp(forward, sequence, *weights)
        gradient = pullback(cotangent_row)
        new_totals = tuple((total_item + grad_item for total_item, grad_item in zip(totals, gradient[1:])))
        return (new_totals, (result.astype(jnp.bfloat16), gradient[0].astype(jnp.bfloat16)))
    zero_sums = tuple((jnp.zeros(w_item.shape, jnp.float32) for w_item in weights))
    totals, (outputs, input_grads) = lax.scan(per_sequence, zero_sums, (tokens.astype(jnp.float32), cotangent.astype(jnp.float32)))
    return (outputs, input_grads, totals[0], totals[1], totals[2], totals[3], totals[4], totals[5], totals[6], totals[7], totals[8])
```

```python
import functools
import math

import jax
import jax.numpy as jnp
from jax import lax
from jax.experimental import pallas as pl
from jax.experimental.pallas import tpu as pltpu
from jax.sharding import PartitionSpec as P

QUERY_HEADS = 9
KEY_VALUE_HEADS = 3
HEAD_DIMENSION = 64


eps = 1e-05
rope_base = 100000.0
mask_fill_value = -1e30


def row_positions(row_ids, block_order, half_size):
    slot_ids = jnp.arange(block_order.shape[0], dtype=jnp.int32)
    chosen = jnp.sum(
        jnp.where((row_ids // half_size)[:, None] == slot_ids[None, :], block_order[None, :], 0),
        axis=1,
    )
    return chosen * half_size + row_ids % half_size


def rope_tables(token_positions):
    inverse = jnp.exp(
        jnp.arange(HEAD_DIMENSION // 2, dtype=jnp.float32)
        * (-2.0 * math.log(rope_base) / HEAD_DIMENSION)
    )
    angles = token_positions.astype(jnp.float32)[:, None] * inverse[None, :]
    return (jnp.cos(angles), jnp.sin(angles))


def apply_rotary(vectors, cosine_table, sine_table):
    front = vectors[..., : HEAD_DIMENSION // 2]
    back_half = vectors[..., HEAD_DIMENSION // 2 :]
    cos_rows = cosine_table[:, None, :]
    sin_rows = sine_table[:, None, :]
    return jnp.concatenate(
        [front * cos_rows - back_half * sin_rows, back_half * cos_rows + front * sin_rows], axis=-1
    )


def rms_scale(values_in):
    return lax.rsqrt(jnp.mean(values_in * values_in, axis=-1, keepdims=True) + eps)


def norm_back(grad_normed, base_rows, gain_rows, scale_rows):
    scaled = grad_normed * gain_rows
    return scale_rows * (scaled - base_rows * jnp.mean(scaled * base_rows, axis=-1, keepdims=True))


def chunk_rows(count):
    return 1024 if count % 1024 == 0 else count


def run_chunks(count, step_fn, carried):
    if count == 1:
        return step_fn(0, carried)
    return lax.fori_loop(0, count, step_fn, carried)


def heads_row(transposed, group):
    width = HEAD_DIMENSION
    return jnp.concatenate(
        [transposed[(group * 3 + g) * width : (group * 3 + g + 1) * width] for g in range(3)],
        axis=1,
    )


def forward_kernel(q_ref, kv_ref, qpos_ref, kpos_ref, mixed_ref, lse_ref, out_scr):
    rows = q_ref.shape[1]
    keys = kv_ref.shape[1]
    width = HEAD_DIMENSION
    size = chunk_rows(keys)
    q_all = q_ref[0].astype(jnp.float32).T.astype(jnp.bfloat16)
    qpos = qpos_ref[...]
    qpos3 = jnp.concatenate([qpos, qpos, qpos], axis=1)
    for group in range(KEY_VALUE_HEADS):
        qt = heads_row(q_all, group)

        def step(c, carried):
            start = c * size
            k = kv_ref[0, pl.ds(start, size), group * width : (group + 1) * width]
            v = kv_ref[0, pl.ds(start, size), (3 + group) * width : (4 + group) * width]
            allowed = kpos_ref[pl.ds(start, size), :] <= qpos3
            scores = jnp.dot(k, qt, preferred_element_type=jnp.float32)
            masked = jnp.where(allowed, scores, mask_fill_value)
            top, total, accum = carried
            new_top = jnp.maximum(top, jnp.max(masked, axis=0, keepdims=True))
            exponent = jnp.exp(masked - new_top)
            factor = jnp.exp(top - new_top)
            part = lax.dot_general(
                v,
                exponent.astype(jnp.bfloat16),
                (((0,), (0,)), ((), ())),
                preferred_element_type=jnp.float32,
            )
            return (
                new_top,
                total * factor + jnp.sum(exponent, axis=0, keepdims=True),
                accum * factor + part,
            )

        top, total, accum = run_chunks(
            keys // size,
            step,
            (
                jnp.full((1, 3 * rows), mask_fill_value, jnp.float32),
                jnp.zeros((1, 3 * rows), jnp.float32),
                jnp.zeros((width, 3 * rows), jnp.float32),
            ),
        )
        attended = accum / total
        lse = top + jnp.log(total)
        for g in range(3):
            head = group * 3 + g
            out_scr[head * width : (head + 1) * width, :] = attended[:, g * rows : (g + 1) * rows]
            lse_ref[0, head : head + 1, :] = lse[:, g * rows : (g + 1) * rows]
    mixed_ref[0] = out_scr[...].T.astype(jnp.bfloat16)


def backward_kernel(
    q_ref, kv_ref, do_ref, mixed_ref, lse_ref, qpos_ref, kpos_ref, dq_ref, dkv_ref, dq_scr
):
    rows = q_ref.shape[1]
    keys = kv_ref.shape[1]
    width = HEAD_DIMENSION
    size = chunk_rows(keys)
    q_rows = q_ref[0]
    do_rows = do_ref[0]
    q_all = q_rows.astype(jnp.float32).T.astype(jnp.bfloat16)
    do_wide = do_rows.astype(jnp.float32).T
    do_all = do_wide.astype(jnp.bfloat16)
    product = do_wide * mixed_ref[0].astype(jnp.float32).T
    qpos = qpos_ref[...]
    qpos3 = jnp.concatenate([qpos, qpos, qpos], axis=1)
    for group in range(KEY_VALUE_HEADS):
        qt = heads_row(q_all, group)
        dot = heads_row(do_all, group)
        delta = jnp.sum(heads_row(product, group), axis=0, keepdims=True)
        lse = jnp.concatenate(
            [lse_ref[0, group * 3 + g : group * 3 + g + 1, :] for g in range(3)], axis=1
        )
        first = group * 3 * width
        q = jnp.concatenate(
            [q_rows[:, first + g * width : first + (g + 1) * width] for g in range(3)], axis=0
        )
        do = jnp.concatenate(
            [do_rows[:, first + g * width : first + (g + 1) * width] for g in range(3)], axis=0
        )

        def step(c, dq):
            start = c * size
            k = kv_ref[0, pl.ds(start, size), group * width : (group + 1) * width]
            v = kv_ref[0, pl.ds(start, size), (3 + group) * width : (4 + group) * width]
            allowed = kpos_ref[pl.ds(start, size), :] <= qpos3
            scores = jnp.dot(k, qt, preferred_element_type=jnp.float32)
            p = jnp.exp(jnp.where(allowed, scores - lse, mask_fill_value))
            dp = jnp.dot(v, dot, preferred_element_type=jnp.float32)
            ds = (p * (dp - delta)).astype(jnp.bfloat16)
            dkv_ref[0, pl.ds(start, size), (3 + group) * width : (4 + group) * width] = jnp.dot(
                p.astype(jnp.bfloat16), do, preferred_element_type=jnp.float32
            ).astype(jnp.bfloat16)
            dkv_ref[0, pl.ds(start, size), group * width : (group + 1) * width] = jnp.dot(
                ds, q, preferred_element_type=jnp.float32
            ).astype(jnp.bfloat16)
            return dq + lax.dot_general(
                k, ds, (((0,), (0,)), ((), ())), preferred_element_type=jnp.float32
            )

        dq = run_chunks(keys // size, step, jnp.zeros((width, 3 * rows), jnp.float32))
        for g in range(3):
            head = group * 3 + g
            dq_scr[head * width : (head + 1) * width, :] = dq[:, g * rows : (g + 1) * rows]
    dq_ref[0] = dq_scr[...].T


def seq_spec(rows, columns):
    return pl.BlockSpec((1, rows, columns), lambda s: (s, 0, 0))


def flat_spec(rows, columns):
    return pl.BlockSpec((rows, columns), lambda s: (0, 0))


def attend(q, kv, qpos, kpos):
    seqs, rows, wide = q.shape
    keys, both = kv.shape[1:]
    return pl.pallas_call(
        forward_kernel,
        grid=(seqs,),
        in_specs=[seq_spec(rows, wide), seq_spec(keys, both), flat_spec(1, rows), flat_spec(keys, 1)],
        out_specs=[seq_spec(rows, wide), seq_spec(16, rows)],
        out_shape=[
            jax.ShapeDtypeStruct((seqs, rows, wide), jnp.bfloat16),
            jax.ShapeDtypeStruct((seqs, 16, rows), jnp.float32),
        ],
        scratch_shapes=[pltpu.VMEM((wide, rows), jnp.float32)],
        compiler_params=pltpu.CompilerParams(vmem_limit_bytes=56 << 20),
        cost_estimate=pl.CostEstimate(
            flops=4 * seqs * rows * wide * keys * 3, bytes_accessed=kv.size * 2, transcendentals=0
        ),
    )(q, kv, qpos, kpos)


def attend_back(q, kv, grad, mixed, lse, qpos, kpos):
    seqs, rows, wide = q.shape
    keys, both = kv.shape[1:]
    return pl.pallas_call(
        backward_kernel,
        grid=(seqs,),
        in_specs=[
            seq_spec(rows, wide),
            seq_spec(keys, both),
            seq_spec(rows, wide),
            seq_spec(rows, wide),
            seq_spec(16, rows),
            flat_spec(1, rows),
            flat_spec(keys, 1),
        ],
        out_specs=[seq_spec(rows, wide), seq_spec(keys, both)],
        out_shape=[
            jax.ShapeDtypeStruct((seqs, rows, wide), jnp.float32),
            jax.ShapeDtypeStruct((seqs, keys, both), jnp.bfloat16),
        ],
        scratch_shapes=[pltpu.VMEM((wide, rows), jnp.float32)],
        compiler_params=pltpu.CompilerParams(vmem_limit_bytes=56 << 20),
        cost_estimate=pl.CostEstimate(
            flops=10 * seqs * rows * wide * keys * 3, bytes_accessed=kv.size * 4, transcendentals=0
        ),
    )(q, kv, grad, mixed, lse, qpos, kpos)


def exchange_kernel(axis, count, source, target, x_ref, o_ref, send_sem, recv_sem, local_sem):
    me = lax.axis_index(axis)
    barrier = pltpu.get_barrier_semaphore()
    for hop in range(1, count):
        pl.semaphore_signal(
            barrier,
            inc=1,
            device_id={axis: lax.rem(me + hop, count)},
            device_id_type=pl.DeviceIdType.MESH,
        )
    own = pltpu.make_async_copy(source(x_ref, me), target(o_ref, me), local_sem)
    own.start()
    pl.semaphore_wait(barrier, count - 1)
    copies = []
    for hop in range(1, count):
        peer = lax.rem(me + hop, count)
        copy = pltpu.make_async_remote_copy(
            src_ref=source(x_ref, peer),
            dst_ref=target(o_ref, me),
            send_sem=send_sem.at[hop],
            recv_sem=recv_sem.at[hop],
            device_id={axis: peer},
            device_id_type=pl.DeviceIdType.MESH,
        )
        copy.start()
        copies.append(copy)
    own.wait()
    for copy in copies:
        copy.wait()


def exchange(x, axis, count, source, target, out_dims, collective_id):
    return pl.pallas_call(
        functools.partial(exchange_kernel, axis, count, source, target),
        in_specs=[pl.BlockSpec(memory_space=pl.ANY)],
        out_specs=pl.BlockSpec(memory_space=pl.ANY),
        out_shape=jax.ShapeDtypeStruct(out_dims, x.dtype),
        scratch_shapes=[
            pltpu.SemaphoreType.DMA((count,)),
            pltpu.SemaphoreType.DMA((count,)),
            pltpu.SemaphoreType.DMA,
        ],
        compiler_params=pltpu.CompilerParams(collective_id=collective_id, has_side_effects=True),
    )(x)


def gather_rows(x, axis, collective_id):
    count, rows = lax.axis_size(axis), x.shape[0]
    return exchange(
        x,
        axis,
        count,
        lambda ref, peer: ref,
        lambda ref, me: ref.at[pl.ds(pl.multiple_of(me * rows, 16), rows)],
        (count * rows,) + x.shape[1:],
        collective_id,
    )


def gather_keys(x, collective_id):
    count, rows = lax.axis_size("ctx"), x.shape[1]
    return exchange(
        x,
        "ctx",
        count,
        lambda ref, peer: ref,
        lambda ref, me: ref.at[:, pl.ds(pl.multiple_of(me * rows, 16), rows)],
        (x.shape[0], count * rows, x.shape[2]),
        collective_id,
    )


def reduce_keys(x, collective_id):
    count = lax.axis_size("ctx")
    rows = x.shape[1] // count
    parts = exchange(
        x,
        "ctx",
        count,
        lambda ref, peer: ref.at[:, pl.ds(pl.multiple_of(peer * rows, 16), rows)],
        lambda ref, me: ref.at[me],
        (count, x.shape[0], rows, x.shape[2]),
        collective_id,
    )
    return jnp.sum(parts.astype(jnp.float32), axis=0)


def gather_shares(x):
    count, rows = lax.axis_size("ctx"), x.shape[0]
    if rows % count:
        return lax.all_gather(x, "fsdp", axis=0, tiled=True)
    share = lax.dynamic_slice_in_dim(x, lax.axis_index("ctx") * (rows // count), rows // count, 0)
    along = lax.all_gather(share, "fsdp", axis=0, tiled=False)
    whole = lax.all_gather(along, "ctx", axis=1, tiled=False)
    return whole.reshape((-1,) + x.shape[1:])


def reduce_rows(x):
    count, parts = lax.axis_size("ctx"), lax.axis_size("fsdp")
    rows = x.shape[0] // parts
    x = x.astype(jnp.bfloat16)
    if rows % count:
        return lax.psum(
            lax.psum_scatter(x, "fsdp", scatter_dimension=0, tiled=True), "ctx"
        ).astype(jnp.float32)
    x = x.reshape((parts, count, rows // count) + x.shape[1:])
    x = lax.psum_scatter(x, "ctx", scatter_dimension=1, tiled=False)
    x = lax.psum_scatter(x, "fsdp", scatter_dimension=0, tiled=False)
    return lax.all_gather(x, "ctx", axis=0, tiled=True).astype(jnp.float32)

def body(
    tokens,
    block_order,
    gain_one,
    gain_two,
    query_weight,
    key_matrix,
    value_matrix,
    out_weight,
    gate_weight,
    up_weight,
    down_weight,
    cotangent,
):
    count_of_sequences, rows_per_block, model_width = tokens.shape
    half_size = rows_per_block // 2
    score_scale = HEAD_DIMENSION ** (-0.5)
    ctx_index = lax.axis_index("ctx")
    first_pack = gather_rows(
        jnp.concatenate([query_weight, key_matrix, value_matrix], axis=1), "fsdp", 0
    )
    kv_width = KEY_VALUE_HEADS * HEAD_DIMENSION
    query_width = query_weight.shape[1]
    ff_width = gate_weight.shape[1]
    gains = lax.all_gather(jnp.stack([gain_one, gain_two]), "fsdp", axis=1, tiled=True)
    second_pack = gather_shares(jnp.concatenate([out_weight, gate_weight, up_weight], axis=1))
    gathered = (
        gains[0],
        gains[1],
        first_pack[:, :query_width],
        first_pack[:, query_width : query_width + kv_width],
        first_pack[:, query_width + kv_width :],
        second_pack[:, :model_width],
        second_pack[:, model_width : model_width + ff_width],
        second_pack[:, model_width + ff_width :],
        gather_shares(down_weight),
    )
    gain_first = gathered[0].astype(jnp.float32)
    gain_second = gathered[1].astype(jnp.float32)
    query_full, key_full, value_full, out_full, gate_full, up_full, down_full = gathered[2:]
    own_positions = row_positions(
        ctx_index * rows_per_block + jnp.arange(rows_per_block, dtype=jnp.int32),
        block_order,
        half_size,
    )
    cosine_table, sine_table = rope_tables(own_positions)
    inputs = tokens.astype(jnp.float32)
    scale_one = rms_scale(inputs)
    base_one = inputs * scale_one
    normed = (base_one * gain_first).astype(jnp.bfloat16)
    query_rows_all = jnp.dot(normed, query_full, preferred_element_type=jnp.float32).reshape(
        count_of_sequences, rows_per_block, QUERY_HEADS, HEAD_DIMENSION
    )
    projected_key = jnp.dot(normed, key_full, preferred_element_type=jnp.float32).reshape(
        count_of_sequences, rows_per_block, KEY_VALUE_HEADS, HEAD_DIMENSION
    )
    projected_value = jnp.dot(normed, value_full, preferred_element_type=jnp.float32).astype(
        jnp.bfloat16
    )
    scaled_query = (
        (apply_rotary(query_rows_all, cosine_table, sine_table).astype(jnp.bfloat16) * score_scale)
        .astype(jnp.bfloat16)
        .reshape(count_of_sequences, rows_per_block, QUERY_HEADS * HEAD_DIMENSION)
    )
    rotary_key = (
        apply_rotary(projected_key, cosine_table, sine_table)
        .astype(jnp.bfloat16)
        .reshape(count_of_sequences, rows_per_block, KEY_VALUE_HEADS * HEAD_DIMENSION)
    )
    key_value = gather_keys(jnp.concatenate([rotary_key, projected_value], axis=-1), 1)
    key_positions = row_positions(
        jnp.arange(key_value.shape[1], dtype=jnp.int32), block_order, half_size
    )[:, None]
    query_positions = own_positions[None, :]
    mixed_heads, log_total = attend(scaled_query, key_value, query_positions, key_positions)
    middle = inputs + jnp.dot(mixed_heads, out_full, preferred_element_type=jnp.float32)
    scale_two = rms_scale(middle)
    base_two = middle * scale_two
    normed_two = (base_two * gain_second).astype(jnp.bfloat16)
    gate_proj = jnp.dot(normed_two, gate_full, preferred_element_type=jnp.float32)
    up_proj = jnp.dot(normed_two, up_full, preferred_element_type=jnp.float32)
    sigmoid_gate = jax.nn.sigmoid(gate_proj)
    activated = gate_proj * sigmoid_gate
    hidden = (activated * up_proj).astype(jnp.bfloat16)
    output = (middle + jnp.dot(hidden, down_full, preferred_element_type=jnp.float32)).astype(
        jnp.bfloat16
    )
    down_grad = jnp.einsum("sbf,sbd->fd", hidden, cotangent, preferred_element_type=jnp.float32)
    grad_hidden = jnp.einsum(
        "sbd,fd->sbf", cotangent, down_full, preferred_element_type=jnp.float32
    )
    grad_gate = (
        grad_hidden * up_proj * sigmoid_gate * (1.0 + gate_proj * (1.0 - sigmoid_gate))
    ).astype(jnp.bfloat16)
    grad_up = (grad_hidden * activated).astype(jnp.bfloat16)
    gate_grad = jnp.einsum("sbd,sbf->df", normed_two, grad_gate, preferred_element_type=jnp.float32)
    up_grad = jnp.einsum("sbd,sbf->df", normed_two, grad_up, preferred_element_type=jnp.float32)
    grad_normed_two = jnp.einsum(
        "sbf,df->sbd", grad_gate, gate_full, preferred_element_type=jnp.float32
    ) + jnp.einsum("sbf,df->sbd", grad_up, up_full, preferred_element_type=jnp.float32)
    gain_two_grad = jnp.sum(grad_normed_two * base_two, axis=(0, 1))
    grad_middle = cotangent.astype(jnp.float32) + norm_back(
        grad_normed_two, base_two, gain_second, scale_two
    )
    grad_branch = grad_middle.astype(jnp.bfloat16)
    out_grad = jnp.einsum(
        "sbq,sbd->qd", mixed_heads, grad_branch, preferred_element_type=jnp.float32
    )
    mixed_gradient = jnp.einsum(
        "sbd,qd->sbq", grad_branch, out_full, preferred_element_type=jnp.float32
    ).astype(jnp.bfloat16)
    owned_down = reduce_rows(down_grad)
    owned_early = reduce_rows(
        jnp.concatenate([out_grad, gate_grad, up_grad, gain_two_grad[:, None]], axis=1)
    )
    query_sum, key_value_part = attend_back(
        scaled_query,
        key_value,
        mixed_gradient,
        mixed_heads,
        log_total,
        query_positions,
        key_positions,
    )
    query_sum = query_sum * score_scale
    grad_query = (
        apply_rotary(
            query_sum.reshape(count_of_sequences, rows_per_block, QUERY_HEADS, HEAD_DIMENSION),
            cosine_table,
            -sine_table,
        )
        .astype(jnp.bfloat16)
        .reshape(count_of_sequences, rows_per_block, QUERY_HEADS * HEAD_DIMENSION)
    )

    key_value_sum = reduce_keys(key_value_part, 2)
    key_sum = key_value_sum[..., :kv_width].reshape(
        count_of_sequences, rows_per_block, KEY_VALUE_HEADS, HEAD_DIMENSION
    )
    grad_key = (
        apply_rotary(key_sum, cosine_table, -sine_table)
        .astype(jnp.bfloat16)
        .reshape(count_of_sequences, rows_per_block, kv_width)
    )
    value_gradient = key_value_sum[..., kv_width:].astype(jnp.bfloat16)
    query_grad = jnp.einsum("sbd,sbq->dq", normed, grad_query, preferred_element_type=jnp.float32)
    key_grad = jnp.einsum("sbd,sbq->dq", normed, grad_key, preferred_element_type=jnp.float32)
    value_grad = jnp.einsum(
        "sbd,sbq->dq", normed, value_gradient, preferred_element_type=jnp.float32
    )
    grad_normed = jnp.einsum(
        "sbq,dq->sbd", grad_query, query_full, preferred_element_type=jnp.float32
    )
    grad_normed = grad_normed + jnp.einsum(
        "sbq,dq->sbd", grad_key, key_full, preferred_element_type=jnp.float32
    )
    grad_normed = grad_normed + jnp.einsum(
        "sbq,dq->sbd", value_gradient, value_full, preferred_element_type=jnp.float32
    )
    gain_one_grad = jnp.sum(grad_normed * base_one, axis=(0, 1))
    grad_tokens = (grad_middle + norm_back(grad_normed, base_one, gain_first, scale_one)).astype(
        jnp.bfloat16
    )
    owned_late = reduce_rows(
        jnp.concatenate([query_grad, key_grad, value_grad, gain_one_grad[:, None]], axis=1)
    )
    owned = (
        owned_late[:, -1],
        owned_early[:, -1],
        owned_late[:, :query_width],
        owned_late[:, query_width : query_width + kv_width],
        owned_late[:, query_width + kv_width : query_width + 2 * kv_width],
        owned_early[:, :model_width],
        owned_early[:, model_width : model_width + ff_width],
        owned_early[:, model_width + ff_width : model_width + 2 * ff_width],
        owned_down,
    )
    return (output, grad_tokens) + tuple(owned)


def solution(mesh):
    return jax.shard_map(
        body,
        mesh=mesh,
        in_specs=(
            P("fsdp", "ctx", None),
            P(),
            P("fsdp"),
            P("fsdp"),
            P("fsdp", None),
            P("fsdp", None),
            P("fsdp", None),
            P("fsdp", None),
            P("fsdp", None),
            P("fsdp", None),
            P("fsdp", None),
            P("fsdp", "ctx", None),
        ),
        out_specs=(
            P("fsdp", "ctx", None),
            P("fsdp", "ctx", None),
            P("fsdp"),
            P("fsdp"),
            P("fsdp", None),
            P("fsdp", None),
            P("fsdp", None),
            P("fsdp", None),
            P("fsdp", None),
            P("fsdp", None),
            P("fsdp", None),
        ),
        check_vma=False,
    )
```

```python
import functools
import math

import jax
import jax.numpy as jnp
from jax import lax
from jax.experimental import pallas as pl
from jax.experimental.pallas import tpu as pltpu
from jax.sharding import PartitionSpec as P

QUERY_HEADS = 9
KEY_VALUE_HEADS = 3
HEAD_DIMENSION = 64


eps = 1e-05
rope_base = 100000.0
mask_fill_value = -1e30


def row_positions(row_ids, block_order, half_size):
    slot_ids = jnp.arange(block_order.shape[0], dtype=jnp.int32)
    chosen = jnp.sum(
        jnp.where((row_ids // half_size)[:, None] == slot_ids[None, :], block_order[None, :], 0),
        axis=1,
    )
    return chosen * half_size + row_ids % half_size


def rope_tables(token_positions):
    inverse = jnp.exp(
        jnp.arange(HEAD_DIMENSION // 2, dtype=jnp.float32)
        * (-2.0 * math.log(rope_base) / HEAD_DIMENSION)
    )
    angles = token_positions.astype(jnp.float32)[:, None] * inverse[None, :]
    return (jnp.cos(angles), jnp.sin(angles))


def apply_rotary(vectors, cosine_table, sine_table):
    front = vectors[..., : HEAD_DIMENSION // 2]
    back_half = vectors[..., HEAD_DIMENSION // 2 :]
    cos_rows = cosine_table[:, None, :]
    sin_rows = sine_table[:, None, :]
    return jnp.concatenate(
        [front * cos_rows - back_half * sin_rows, back_half * cos_rows + front * sin_rows], axis=-1
    )


def rms_scale(values_in):
    return lax.rsqrt(jnp.mean(values_in * values_in, axis=-1, keepdims=True) + eps)


def norm_back(grad_normed, base_rows, gain_rows, scale_rows):
    scaled = grad_normed * gain_rows
    return scale_rows * (scaled - base_rows * jnp.mean(scaled * base_rows, axis=-1, keepdims=True))


def chunk_rows(count):
    return 1024 if count % 1024 == 0 else count


def run_chunks(count, step_fn, carried):
    if count == 1:
        return step_fn(0, carried)
    return lax.fori_loop(0, count, step_fn, carried)


def heads_row(transposed, group):
    width = HEAD_DIMENSION
    return jnp.concatenate(
        [transposed[(group * 3 + g) * width : (group * 3 + g + 1) * width] for g in range(3)],
        axis=1,
    )


def forward_kernel(q_ref, kv_ref, qpos_ref, kpos_ref, mixed_ref, lse_ref, out_scr):
    rows = q_ref.shape[1]
    keys = kv_ref.shape[1]
    width = HEAD_DIMENSION
    size = chunk_rows(keys)
    q_all = q_ref[0].astype(jnp.float32).T.astype(jnp.bfloat16)
    qpos = qpos_ref[...]
    qpos3 = jnp.concatenate([qpos, qpos, qpos], axis=1)
    for group in range(KEY_VALUE_HEADS):
        qt = heads_row(q_all, group)

        def step(c, carried):
            start = c * size
            k = kv_ref[0, pl.ds(start, size), group * width : (group + 1) * width]
            v = kv_ref[0, pl.ds(start, size), (3 + group) * width : (4 + group) * width]
            allowed = kpos_ref[pl.ds(start, size), :] <= qpos3
            scores = jnp.dot(k, qt, preferred_element_type=jnp.float32)
            masked = jnp.where(allowed, scores, mask_fill_value)
            top, total, accum = carried
            new_top = jnp.maximum(top, jnp.max(masked, axis=0, keepdims=True))
            exponent = jnp.exp(masked - new_top)
            factor = jnp.exp(top - new_top)
            part = lax.dot_general(
                v,
                exponent.astype(jnp.bfloat16),
                (((0,), (0,)), ((), ())),
                preferred_element_type=jnp.float32,
            )
            return (
                new_top,
                total * factor + jnp.sum(exponent, axis=0, keepdims=True),
                accum * factor + part,
            )

        top, total, accum = run_chunks(
            keys // size,
            step,
            (
                jnp.full((1, 3 * rows), mask_fill_value, jnp.float32),
                jnp.zeros((1, 3 * rows), jnp.float32),
                jnp.zeros((width, 3 * rows), jnp.float32),
            ),
        )
        attended = accum / total
        lse = top + jnp.log(total)
        for g in range(3):
            head = group * 3 + g
            out_scr[head * width : (head + 1) * width, :] = attended[:, g * rows : (g + 1) * rows]
            lse_ref[0, head : head + 1, :] = lse[:, g * rows : (g + 1) * rows]
    mixed_ref[0] = out_scr[...].T.astype(jnp.bfloat16)


def backward_kernel(
    q_ref, kv_ref, do_ref, mixed_ref, lse_ref, qpos_ref, kpos_ref, dq_ref, dkv_ref, dq_scr
):
    rows = q_ref.shape[1]
    keys = kv_ref.shape[1]
    width = HEAD_DIMENSION
    size = chunk_rows(keys)
    q_rows = q_ref[0]
    do_rows = do_ref[0]
    q_all = q_rows.astype(jnp.float32).T.astype(jnp.bfloat16)
    do_wide = do_rows.astype(jnp.float32).T
    do_all = do_wide.astype(jnp.bfloat16)
    product = do_wide * mixed_ref[0].astype(jnp.float32).T
    qpos = qpos_ref[...]
    qpos3 = jnp.concatenate([qpos, qpos, qpos], axis=1)
    for group in range(KEY_VALUE_HEADS):
        qt = heads_row(q_all, group)
        dot = heads_row(do_all, group)
        delta = jnp.sum(heads_row(product, group), axis=0, keepdims=True)
        lse = jnp.concatenate(
            [lse_ref[0, group * 3 + g : group * 3 + g + 1, :] for g in range(3)], axis=1
        )
        first = group * 3 * width
        q = jnp.concatenate(
            [q_rows[:, first + g * width : first + (g + 1) * width] for g in range(3)], axis=0
        )
        do = jnp.concatenate(
            [do_rows[:, first + g * width : first + (g + 1) * width] for g in range(3)], axis=0
        )

        def step(c, dq):
            start = c * size
            k = kv_ref[0, pl.ds(start, size), group * width : (group + 1) * width]
            v = kv_ref[0, pl.ds(start, size), (3 + group) * width : (4 + group) * width]
            allowed = kpos_ref[pl.ds(start, size), :] <= qpos3
            scores = jnp.dot(k, qt, preferred_element_type=jnp.float32)
            p = jnp.exp(jnp.where(allowed, scores - lse, mask_fill_value))
            dp = jnp.dot(v, dot, preferred_element_type=jnp.float32)
            ds = (p * (dp - delta)).astype(jnp.bfloat16)
            dkv_ref[0, pl.ds(start, size), (3 + group) * width : (4 + group) * width] = jnp.dot(
                p.astype(jnp.bfloat16), do, preferred_element_type=jnp.float32
            ).astype(jnp.bfloat16)
            dkv_ref[0, pl.ds(start, size), group * width : (group + 1) * width] = jnp.dot(
                ds, q, preferred_element_type=jnp.float32
            ).astype(jnp.bfloat16)
            return dq + lax.dot_general(
                k, ds, (((0,), (0,)), ((), ())), preferred_element_type=jnp.float32
            )

        dq = run_chunks(keys // size, step, jnp.zeros((width, 3 * rows), jnp.float32))
        for g in range(3):
            head = group * 3 + g
            dq_scr[head * width : (head + 1) * width, :] = dq[:, g * rows : (g + 1) * rows]
    dq_ref[0] = dq_scr[...].T


def seq_spec(rows, columns):
    return pl.BlockSpec((1, rows, columns), lambda s: (s, 0, 0))


def flat_spec(rows, columns):
    return pl.BlockSpec((rows, columns), lambda s: (0, 0))


def attend(q, kv, qpos, kpos):
    seqs, rows, wide = q.shape
    keys, both = kv.shape[1:]
    return pl.pallas_call(
        forward_kernel,
        grid=(seqs,),
        in_specs=[seq_spec(rows, wide), seq_spec(keys, both), flat_spec(1, rows), flat_spec(keys, 1)],
        out_specs=[seq_spec(rows, wide), seq_spec(16, rows)],
        out_shape=[
            jax.ShapeDtypeStruct((seqs, rows, wide), jnp.bfloat16),
            jax.ShapeDtypeStruct((seqs, 16, rows), jnp.float32),
        ],
        scratch_shapes=[pltpu.VMEM((wide, rows), jnp.float32)],
        compiler_params=pltpu.CompilerParams(vmem_limit_bytes=56 << 20),
        cost_estimate=pl.CostEstimate(
            flops=4 * seqs * rows * wide * keys * 3, bytes_accessed=kv.size * 2, transcendentals=0
        ),
    )(q, kv, qpos, kpos)


def attend_back(q, kv, grad, mixed, lse, qpos, kpos):
    seqs, rows, wide = q.shape
    keys, both = kv.shape[1:]
    return pl.pallas_call(
        backward_kernel,
        grid=(seqs,),
        in_specs=[
            seq_spec(rows, wide),
            seq_spec(keys, both),
            seq_spec(rows, wide),
            seq_spec(rows, wide),
            seq_spec(16, rows),
            flat_spec(1, rows),
            flat_spec(keys, 1),
        ],
        out_specs=[seq_spec(rows, wide), seq_spec(keys, both)],
        out_shape=[
            jax.ShapeDtypeStruct((seqs, rows, wide), jnp.float32),
            jax.ShapeDtypeStruct((seqs, keys, both), jnp.bfloat16),
        ],
        scratch_shapes=[pltpu.VMEM((wide, rows), jnp.float32)],
        compiler_params=pltpu.CompilerParams(vmem_limit_bytes=56 << 20),
        cost_estimate=pl.CostEstimate(
            flops=10 * seqs * rows * wide * keys * 3, bytes_accessed=kv.size * 4, transcendentals=0
        ),
    )(q, kv, grad, mixed, lse, qpos, kpos)


def exchange_kernel(axis, count, source, target, x_ref, o_ref, send_sem, recv_sem, local_sem):
    me = lax.axis_index(axis)
    barrier = pltpu.get_barrier_semaphore()
    for hop in range(1, count):
        pl.semaphore_signal(
            barrier,
            inc=1,
            device_id={axis: lax.rem(me + hop, count)},
            device_id_type=pl.DeviceIdType.MESH,
        )
    own = pltpu.make_async_copy(source(x_ref, me), target(o_ref, me), local_sem)
    own.start()
    pl.semaphore_wait(barrier, count - 1)
    copies = []
    for hop in range(1, count):
        peer = lax.rem(me + hop, count)
        copy = pltpu.make_async_remote_copy(
            src_ref=source(x_ref, peer),
            dst_ref=target(o_ref, me),
            send_sem=send_sem.at[hop],
            recv_sem=recv_sem.at[hop],
            device_id={axis: peer},
            device_id_type=pl.DeviceIdType.MESH,
        )
        copy.start()
        copies.append(copy)
    own.wait()
    for copy in copies:
        copy.wait()


def exchange(x, axis, count, source, target, out_dims, collective_id):
    return pl.pallas_call(
        functools.partial(exchange_kernel, axis, count, source, target),
        in_specs=[pl.BlockSpec(memory_space=pl.ANY)],
        out_specs=pl.BlockSpec(memory_space=pl.ANY),
        out_shape=jax.ShapeDtypeStruct(out_dims, x.dtype),
        scratch_shapes=[
            pltpu.SemaphoreType.DMA((count,)),
            pltpu.SemaphoreType.DMA((count,)),
            pltpu.SemaphoreType.DMA,
        ],
        compiler_params=pltpu.CompilerParams(collective_id=collective_id, has_side_effects=True),
    )(x)


def gather_rows(x, axis, collective_id):
    count, rows = lax.axis_size(axis), x.shape[0]
    return exchange(
        x,
        axis,
        count,
        lambda ref, peer: ref,
        lambda ref, me: ref.at[pl.ds(pl.multiple_of(me * rows, 16), rows)],
        (count * rows,) + x.shape[1:],
        collective_id,
    )


def gather_keys(x, collective_id):
    count, rows = lax.axis_size("ctx"), x.shape[1]
    return exchange(
        x,
        "ctx",
        count,
        lambda ref, peer: ref,
        lambda ref, me: ref.at[:, pl.ds(pl.multiple_of(me * rows, 16), rows)],
        (x.shape[0], count * rows, x.shape[2]),
        collective_id,
    )


def reduce_keys(x, collective_id):
    count = lax.axis_size("ctx")
    rows = x.shape[1] // count
    parts = exchange(
        x,
        "ctx",
        count,
        lambda ref, peer: ref.at[:, pl.ds(pl.multiple_of(peer * rows, 16), rows)],
        lambda ref, me: ref.at[me],
        (count, x.shape[0], rows, x.shape[2]),
        collective_id,
    )
    return jnp.sum(parts.astype(jnp.float32), axis=0)


def split_columns(matrix):
    count = lax.axis_size("ctx")
    return jnp.moveaxis(matrix.reshape(matrix.shape[0], count, -1), 1, 0)


def join_columns(pieces):
    return jnp.moveaxis(pieces, 0, 1).reshape(pieces.shape[1], -1)


def split_down(matrix, parts, rows):
    count = lax.axis_size("ctx")
    down_rows = matrix.shape[0] // (parts * count)
    groups = rows // down_rows
    pieces = matrix.reshape(parts, count, down_rows, groups, -1)
    return jnp.transpose(pieces, (1, 0, 3, 2, 4)).reshape(count, parts * rows, -1)


def join_down(pieces, parts, down_rows):
    count, rows, width = pieces.shape
    groups = rows // parts // down_rows
    split = pieces.reshape(count, parts, groups, down_rows, width)
    return jnp.transpose(split, (1, 0, 3, 2, 4)).reshape(parts * count * down_rows, -1)


def gather_shares(pieces):
    share = lax.dynamic_index_in_dim(pieces, lax.axis_index("ctx"), 0, keepdims=False)
    along = lax.all_gather(share, "fsdp", axis=0, tiled=True)
    whole = lax.all_gather(along, "ctx", axis=0, tiled=True)
    return whole.reshape((pieces.shape[0], -1) + pieces.shape[2:])


def reduce_pieces(pieces):
    count, rows, width = pieces.shape
    mine = lax.psum_scatter(
        pieces.reshape(count * rows, width), "ctx", scatter_dimension=0, tiled=True
    )
    mine = lax.psum_scatter(mine, "fsdp", scatter_dimension=0, tiled=True)
    return lax.all_gather(mine, "ctx", axis=0, tiled=True).reshape(count, -1, width)


def exchange_sum(pieces, axis, collective_id):
    parts = exchange(
        pieces,
        axis,
        pieces.shape[0],
        lambda ref, peer: ref.at[peer],
        lambda ref, me: ref.at[me],
        pieces.shape,
        collective_id,
    )
    return jnp.sum(parts.astype(jnp.float32), axis=0)


def reduce_pieces_now(pieces, first_id):
    count, rows, width = pieces.shape
    mine = exchange_sum(pieces, "ctx", first_id).astype(jnp.bfloat16)
    parts = lax.axis_size("fsdp")
    mine = exchange_sum(mine.reshape(parts, rows // parts, width), "fsdp", first_id + 1)
    return gather_rows(mine.astype(jnp.bfloat16), "ctx", first_id + 2).reshape(
        count, rows // parts, width
    )

def body(
    tokens,
    block_order,
    gain_one,
    gain_two,
    query_weight,
    key_matrix,
    value_matrix,
    out_weight,
    gate_weight,
    up_weight,
    down_weight,
    cotangent,
):
    count_of_sequences, rows_per_block, model_width = tokens.shape
    half_size = rows_per_block // 2
    score_scale = HEAD_DIMENSION ** (-0.5)
    ctx_index = lax.axis_index("ctx")
    count = lax.axis_size("ctx")
    parts = lax.axis_size("fsdp")
    rows_owned = query_weight.shape[0]
    kv_width = KEY_VALUE_HEADS * HEAD_DIMENSION
    query_width = query_weight.shape[1]
    ff_width = gate_weight.shape[1]
    down_rows = down_weight.shape[0] // count
    down_end = ff_width // count
    gate_end = down_end + ff_width // count
    up_end = gate_end + ff_width // count
    filler = jnp.zeros((rows_owned, -(query_width + 2 * kv_width + 2) % 128), gain_one.dtype)
    first_pack = gather_rows(
        jnp.concatenate(
            [query_weight, key_matrix, value_matrix, gain_one[:, None], gain_two[:, None], filler],
            axis=1,
        ),
        "fsdp",
        0,
    )
    second_pack = gather_shares(
        jnp.concatenate(
            [
                split_down(down_weight, 1, rows_owned),
                split_columns(gate_weight),
                split_columns(up_weight),
                split_columns(out_weight),
            ],
            axis=2,
        )
    )
    gathered = (
        first_pack[:, query_width + 2 * kv_width],
        first_pack[:, query_width + 2 * kv_width + 1],
        first_pack[:, :query_width],
        first_pack[:, query_width : query_width + kv_width],
        first_pack[:, query_width + kv_width : query_width + 2 * kv_width],
        join_columns(second_pack[:, :, up_end:]),
        join_columns(second_pack[:, :, down_end:gate_end]),
        join_columns(second_pack[:, :, gate_end:up_end]),
        join_down(second_pack[:, :, :down_end], parts, down_rows),
    )
    gain_first = gathered[0].astype(jnp.float32)
    gain_second = gathered[1].astype(jnp.float32)
    query_full, key_full, value_full, out_full, gate_full, up_full, down_full = gathered[2:]
    own_positions = row_positions(
        ctx_index * rows_per_block + jnp.arange(rows_per_block, dtype=jnp.int32),
        block_order,
        half_size,
    )
    cosine_table, sine_table = rope_tables(own_positions)
    inputs = tokens.astype(jnp.float32)
    scale_one = rms_scale(inputs)
    base_one = inputs * scale_one
    normed = (base_one * gain_first).astype(jnp.bfloat16)
    query_rows_all = jnp.dot(normed, query_full, preferred_element_type=jnp.float32).reshape(
        count_of_sequences, rows_per_block, QUERY_HEADS, HEAD_DIMENSION
    )
    projected_key = jnp.dot(normed, key_full, preferred_element_type=jnp.float32).reshape(
        count_of_sequences, rows_per_block, KEY_VALUE_HEADS, HEAD_DIMENSION
    )
    projected_value = jnp.dot(normed, value_full, preferred_element_type=jnp.float32).astype(
        jnp.bfloat16
    )
    scaled_query = (
        (apply_rotary(query_rows_all, cosine_table, sine_table).astype(jnp.bfloat16) * score_scale)
        .astype(jnp.bfloat16)
        .reshape(count_of_sequences, rows_per_block, QUERY_HEADS * HEAD_DIMENSION)
    )
    rotary_key = (
        apply_rotary(projected_key, cosine_table, sine_table)
        .astype(jnp.bfloat16)
        .reshape(count_of_sequences, rows_per_block, KEY_VALUE_HEADS * HEAD_DIMENSION)
    )
    key_value = gather_keys(jnp.concatenate([rotary_key, projected_value], axis=-1), 1)
    key_positions = row_positions(
        jnp.arange(key_value.shape[1], dtype=jnp.int32), block_order, half_size
    )[:, None]
    query_positions = own_positions[None, :]
    mixed_heads, log_total = attend(scaled_query, key_value, query_positions, key_positions)
    middle = inputs + jnp.dot(mixed_heads, out_full, preferred_element_type=jnp.float32)
    scale_two = rms_scale(middle)
    base_two = middle * scale_two
    normed_two = (base_two * gain_second).astype(jnp.bfloat16)
    gate_proj = jnp.dot(normed_two, gate_full, preferred_element_type=jnp.float32)
    up_proj = jnp.dot(normed_two, up_full, preferred_element_type=jnp.float32)
    sigmoid_gate = jax.nn.sigmoid(gate_proj)
    activated = gate_proj * sigmoid_gate
    hidden = (activated * up_proj).astype(jnp.bfloat16)
    output = (middle + jnp.dot(hidden, down_full, preferred_element_type=jnp.float32)).astype(
        jnp.bfloat16
    )
    down_grad = jnp.einsum("sbf,sbd->fd", hidden, cotangent, preferred_element_type=jnp.float32)
    grad_hidden = jnp.einsum(
        "sbd,fd->sbf", cotangent, down_full, preferred_element_type=jnp.float32
    )
    grad_gate = (
        grad_hidden * up_proj * sigmoid_gate * (1.0 + gate_proj * (1.0 - sigmoid_gate))
    ).astype(jnp.bfloat16)
    grad_up = (grad_hidden * activated).astype(jnp.bfloat16)
    gate_grad = jnp.einsum("sbd,sbf->df", normed_two, grad_gate, preferred_element_type=jnp.float32)
    up_grad = jnp.einsum("sbd,sbf->df", normed_two, grad_up, preferred_element_type=jnp.float32)
    grad_normed_two = jnp.einsum(
        "sbf,df->sbd", grad_gate, gate_full, preferred_element_type=jnp.float32
    ) + jnp.einsum("sbf,df->sbd", grad_up, up_full, preferred_element_type=jnp.float32)
    gain_two_grad = jnp.sum(grad_normed_two * base_two, axis=(0, 1))
    grad_middle = cotangent.astype(jnp.float32) + norm_back(
        grad_normed_two, base_two, gain_second, scale_two
    )
    grad_branch = grad_middle.astype(jnp.bfloat16)
    out_grad = jnp.einsum(
        "sbq,sbd->qd", mixed_heads, grad_branch, preferred_element_type=jnp.float32
    )
    mixed_gradient = jnp.einsum(
        "sbd,qd->sbq", grad_branch, out_full, preferred_element_type=jnp.float32
    ).astype(jnp.bfloat16)
    bf16 = jnp.bfloat16
    early = reduce_pieces(
        jnp.concatenate(
            [
                split_down(down_grad.astype(bf16), parts, rows_owned),
                split_columns(gate_grad.astype(bf16)),
                split_columns(up_grad.astype(bf16)),
                split_columns(out_grad.astype(bf16)),
            ],
            axis=2,
        )
    ).astype(jnp.float32)
    query_sum, key_value_part = attend_back(
        scaled_query,
        key_value,
        mixed_gradient,
        mixed_heads,
        log_total,
        query_positions,
        key_positions,
    )
    query_sum = query_sum * score_scale
    grad_query = (
        apply_rotary(
            query_sum.reshape(count_of_sequences, rows_per_block, QUERY_HEADS, HEAD_DIMENSION),
            cosine_table,
            -sine_table,
        )
        .astype(jnp.bfloat16)
        .reshape(count_of_sequences, rows_per_block, QUERY_HEADS * HEAD_DIMENSION)
    )

    key_value_sum = reduce_keys(key_value_part, 2)
    key_sum = key_value_sum[..., :kv_width].reshape(
        count_of_sequences, rows_per_block, KEY_VALUE_HEADS, HEAD_DIMENSION
    )
    grad_key = (
        apply_rotary(key_sum, cosine_table, -sine_table)
        .astype(jnp.bfloat16)
        .reshape(count_of_sequences, rows_per_block, kv_width)
    )
    value_gradient = key_value_sum[..., kv_width:].astype(jnp.bfloat16)
    query_grad = jnp.einsum("sbd,sbq->dq", normed, grad_query, preferred_element_type=jnp.float32)
    key_grad = jnp.einsum("sbd,sbq->dq", normed, grad_key, preferred_element_type=jnp.float32)
    value_grad = jnp.einsum(
        "sbd,sbq->dq", normed, value_gradient, preferred_element_type=jnp.float32
    )
    grad_normed = jnp.einsum(
        "sbq,dq->sbd", grad_query, query_full, preferred_element_type=jnp.float32
    )
    grad_normed = grad_normed + jnp.einsum(
        "sbq,dq->sbd", grad_key, key_full, preferred_element_type=jnp.float32
    )
    grad_normed = grad_normed + jnp.einsum(
        "sbq,dq->sbd", value_gradient, value_full, preferred_element_type=jnp.float32
    )
    gain_one_grad = jnp.sum(grad_normed * base_one, axis=(0, 1))
    grad_tokens = (grad_middle + norm_back(grad_normed, base_one, gain_first, scale_one)).astype(
        jnp.bfloat16
    )
    gain_grads = jnp.stack([gain_one_grad, gain_two_grad], axis=1).astype(bf16)
    columns = [split_columns(g.astype(bf16)) for g in (query_grad, key_grad, value_grad)]
    gain_columns = jnp.broadcast_to(gain_grads[None], (count,) + gain_grads.shape)
    used = sum(g.shape[2] for g in columns) + 2
    filler = jnp.zeros((count, model_width, -used % 128), bf16)
    late = reduce_pieces_now(
        jnp.concatenate(columns + [gain_columns, filler], axis=2), 3
    ).astype(jnp.float32)
    query_end = query_width // count
    key_end = query_end + kv_width // count
    value_end = key_end + kv_width // count
    owned = (
        late[0, :, value_end],
        late[0, :, value_end + 1],
        join_columns(late[:, :, :query_end]),
        join_columns(late[:, :, query_end:key_end]),
        join_columns(late[:, :, key_end:value_end]),
        join_columns(early[:, :, up_end:]),
        join_columns(early[:, :, down_end:gate_end]),
        join_columns(early[:, :, gate_end:up_end]),
        join_down(early[:, :, :down_end], 1, down_rows),
    )
    return (output, grad_tokens) + tuple(owned)


def solution(mesh):
    return jax.shard_map(
        body,
        mesh=mesh,
        in_specs=(
            P("fsdp", "ctx", None),
            P(),
            P("fsdp"),
            P("fsdp"),
            P("fsdp", None),
            P("fsdp", None),
            P("fsdp", None),
            P("fsdp", None),
            P("fsdp", None),
            P("fsdp", None),
            P("fsdp", None),
            P("fsdp", "ctx", None),
        ),
        out_specs=(
            P("fsdp", "ctx", None),
            P("fsdp", "ctx", None),
            P("fsdp"),
            P("fsdp"),
            P("fsdp", None),
            P("fsdp", None),
            P("fsdp", None),
            P("fsdp", None),
            P("fsdp", None),
            P("fsdp", None),
            P("fsdp", None),
        ),
        check_vma=False,
    )
```
